32 devices in a mesh: parts: 2 (over y), tensor: 8 (over z, x), dp: 2 (over core).
Axes of the slice: x: 2, y: 2, z: 4, core: 2. Of those that a mesh axis runs over, the one named last changes fastest.
Arguments:
- cotangent: bfloat16 [8192, 2048], P('tensor', ('parts', 'dp')), parts along dimension 1, may hold values from -6 to 6
- layer_input: bfloat16 [8192, 2048], P('tensor', ('parts', 'dp')), parts along dimension 1, may hold values from -6 to 6
- gate_pre: bfloat16 [28672, 2048], P('tensor', ('parts', 'dp')), parts along dimension 1, may hold values from -6 to 6
- up_pre: bfloat16 [28672, 2048], P('tensor', ('parts', 'dp')), parts along dimension 1, may hold values from -6 to 6
- down_weight: bfloat16 [28672, 8192], P('tensor'), may hold values from -0.0625 to 0.0625
- proj_input: bfloat16 [8192, 64], P('tensor'), may hold values from -0.0625 to 0.0625
- proj_gate: bfloat16 [28672, 64], P('tensor'), may hold values from -0.03125 to 0.03125
- proj_up: bfloat16 [28672, 64], P('tensor'), may hold values from -0.03125 to 0.03125
- store_slot: int32 [16], P(('parts', 'dp')), parts along dimension 0, may hold values from 0 to 7, each once
- example_ids: int32 [16], P(('parts', 'dp')), parts along dimension 0, may hold values from 0 to 999999
- lengths: int32 [16], P(('parts', 'dp')), parts along dimension 0, may hold values from 1 to 128, 768 in all
Outputs:
- store_keys: bfloat16 [16, 8192], P(('parts', 'dp')), parts along dimension 0
- store_ids: int32 [16], P(('parts', 'dp')), parts along dimension 0
The draws below stay inside these ranges and needn't reach their ends.
There are 2 independent parts, one for each index of `parts`. The reference program is written for one: setup_inputs(seed, part) draws one part's arguments, and reference() takes and returns one part's arrays. A program takes and returns all parts, laid end to end along the dimension named above; an argument that names none is the same for every part. Nothing has to cross between parts.
Inputs may be any that keep to these rules, and one draw needn't show every extreme that they name: `store_slot`: each of 0 to 7 appears exactly once.
All inputs are finite; a program needn't handle non-finite values. No bound on the sum of `lengths` on one device may be relied on, other than what follows from the above.
Results may differ from the reference program's by a relative error of at most 0.0052.
Values may be sent and summed in bfloat16 or wider, within the bound.
A program may use at most 192 MiB of HBM per device.

```python
import math
import jax
import jax.numpy as jnp
import numpy as np
from jax import lax

D = 8192
FF = 28672
PROJ = 64
LEN = 128
SEQS = 8
TOKENS = 1024


def set_ends(values, key, low, high):
    longest = values.shape.index(max(values.shape))
    spots = []
    for shift in (0, 1):
        where = [jax.random.randint(jax.random.fold_in(key, axis), (), 0, length) for axis, length in enumerate(values.shape)]
        where[longest] = (where[longest] + shift) % values.shape[longest]
        spots.append(tuple(where))
    return values.at[spots[0]].set(low).at[spots[1]].set(high)


def level_of(rng, dims, shards, low, largest):
    level, own = 1.0, jax.random.fold_in(rng, 6)
    for dim, blocks in shards:
        heights = jnp.exp(jax.random.uniform(jax.random.fold_in(own, dim), (blocks,), jnp.float32, low / len(shards), largest / len(shards)))
        level = level * jnp.repeat(heights, dims[dim] // blocks).reshape([-1 if axis == dim else 1 for axis in range(len(dims))])
    return level


def split_up(number_of, total, reach, skew):
    portions = [(1 << 20) // math.isqrt(standing ** skew) + 1 for standing in range(2, number_of + 1)]
    surplus, given = total - reach - (number_of - 1), [1] * (number_of - 1)
    while surplus > 0:
        candidates = [i for i in range(number_of - 1) if given[i] < reach]
        mass, remaining = sum([portions[i] for i in candidates]), surplus
        for i in candidates:
            extra = min(reach - given[i], max(1, remaining * portions[i] // mass), surplus)
            given[i] = given[i] + extra
            surplus = surplus - extra
    return np.array([reach] + given)


def uneven_parts(key, amount, total, most, skew):
    if amount == 2:
        one = jax.random.randint(key, (), max(1, total - most), min(most, total - 1) + 1)
        return jnp.stack([one, total - one])
    tallies = jnp.asarray(split_up(amount, total, most, skew), jnp.int32)
    couples = (amount - 1) // 2
    source_of, taker = tallies[1:1 + 2 * couples:2], tallies[2:2 + 2 * couples:2]
    margin = jnp.minimum(source_of - 1, most - taker)
    shifted = jax.random.randint(jax.random.fold_in(key, 1), (couples,), 0, 1 << 20) % (margin + 1)
    tallies = tallies.at[1:1 + 2 * couples:2].set(source_of - shifted).at[2:2 + 2 * couples:2].set(taker + shifted)
    return tallies[jax.random.permutation(jax.random.fold_in(key, 2), amount)]


def noise(rng, extent, deviation, limit, cuts=(), kind=jnp.bfloat16):
    level = level_of(rng, extent, cuts, -0.22, 0.18) if cuts else 1.0
    drawn = jax.random.normal(rng, extent, jnp.float32) * deviation * level
    return jnp.minimum(jnp.maximum(drawn, -limit), limit).astype(kind)


def setup_inputs(seed: int = 0, part: int = 0) -> dict:
    arg_keys = jax.random.split(jax.random.key(seed), 12)
    part_splits = jax.random.split(jax.random.fold_in(arg_keys[11], part), 12)
    return {
        "cotangent": noise(part_splits[0], (D, TOKENS), 1.0, 6.0, ((0, 8), (1, 2))),
        "layer_input": noise(part_splits[1], (D, TOKENS), 1.0, 6.0, ((0, 8), (1, 2))),
        "gate_pre": noise(part_splits[2], (FF, TOKENS), 1.0, 6.0, ((0, 8), (1, 2))),
        "up_pre": noise(part_splits[3], (FF, TOKENS), 1.0, 6.0, ((0, 8), (1, 2))),
        "down_weight": noise(arg_keys[4], (FF, D), D ** -0.5, 0.0625, ((0, 8),)),
        "proj_input": noise(arg_keys[5], (D, PROJ), D ** -0.5, 0.0625, ((0, 8),)),
        "proj_gate": noise(arg_keys[6], (FF, PROJ), FF ** -0.5, 0.03125, ((0, 8),)),
        "proj_up": noise(arg_keys[7], (FF, PROJ), FF ** -0.5, 0.03125, ((0, 8),)),
        "store_slot": jax.random.permutation(part_splits[8], SEQS).astype(jnp.int32),
        "example_ids": set_ends(jax.random.randint(part_splits[9], (SEQS,), 0, 1000000), jax.random.fold_in(part_splits[9], 1), 0, 999999).astype(jnp.int32),
        "lengths": uneven_parts(part_splits[10], SEQS, SEQS * LEN * 3 // 4, LEN, 1).astype(jnp.int32),
    }


def silu_parts(gate_value):
    sigmoid_gate = jax.nn.sigmoid(gate_value)
    return (gate_value * sigmoid_gate, sigmoid_gate * (1.0 + gate_value * (1.0 - sigmoid_gate)))

def make_keys(grad_rows, input_factor, lengths):
    seq_count = lengths.shape[0]
    proj_rank = input_factor.shape[0]
    seq_len = input_factor.shape[1] // seq_count
    position = jnp.arange(seq_len, dtype=jnp.int32)
    inside = jnp.where(position[None, :] < lengths[:, None], 1.0, 0.0).astype(jnp.float32)
    weight = inside * lax.rsqrt(lengths.astype(jnp.float32))[:, None]
    grads_three = grad_rows.reshape(2, proj_rank, seq_count, seq_len)
    inputs_three = input_factor.reshape(proj_rank, seq_count, seq_len)
    key_rows = jnp.einsum('gael,bel,el->egab', grads_three, inputs_three, weight, precision=lax.Precision.HIGHEST)
    return key_rows.reshape(seq_count, -1).astype(jnp.bfloat16)

def reference(cotangent, layer_input, gate_pre, up_pre, down_weight, proj_input, proj_gate, proj_up, store_slot, example_ids, lengths):
    hidden_grad = jnp.dot(down_weight, cotangent, preferred_element_type=jnp.float32)
    gate_value = gate_pre.astype(jnp.float32)
    up_value = up_pre.astype(jnp.float32)
    activated, slope = silu_parts(gate_value)
    gate_grad = (hidden_grad * up_value * slope).astype(jnp.bfloat16)
    up_grad = (hidden_grad * activated).astype(jnp.bfloat16)
    gate_factor = jnp.dot(proj_gate.T, gate_grad, preferred_element_type=jnp.float32)
    up_factor = jnp.dot(proj_up.T, up_grad, preferred_element_type=jnp.float32)
    input_factor = jnp.dot(proj_input.T, layer_input, preferred_element_type=jnp.float32)
    grad_rows = jnp.concatenate([gate_factor, up_factor], axis=0)
    key_rows = make_keys(grad_rows, input_factor, lengths)
    store_keys = jnp.zeros_like(key_rows).at[store_slot].set(key_rows)
    store_ids = jnp.zeros_like(example_ids).at[store_slot].set(example_ids)
    return (store_keys, store_ids)
```

```python
import functools

import jax
import jax.numpy as jnp
from jax import lax
from jax.experimental import pallas as pl
from jax.experimental.pallas import tpu as pltpu
from jax.sharding import PartitionSpec as P

MESH = pl.DeviceIdType.MESH
F32 = jnp.float32
BF16 = jnp.bfloat16
PIECES = 2
W_SLOTS = 3
ROWS = 512


def silu_parts(gate_value):
    sigmoid_gate = jax.nn.sigmoid(gate_value)
    return (gate_value * sigmoid_gate, sigmoid_gate * (1.0 + gate_value * (1.0 - sigmoid_gate)))


def contract_first(left, right):
    return lax.dot_general(
        left, right, (((0,), (0,)), ((), ())), preferred_element_type=jnp.float32
    )


def contract_last(left, right):
    return lax.dot_general(
        left,
        right,
        (((1,), (1,)), ((), ())),
        precision=lax.Precision.HIGHEST,
        preferred_element_type=jnp.float32,
    )


def keys_kernel(
    cot_ref,
    w_ref,
    gate_ref,
    up_ref,
    pg_ref,
    pu_ref,
    inp_ref,
    mask_ref,
    out_ref,
    held,
    wbuf,
    acc,
    gate_mul,
    up_mul,
    stage,
    irecv,
    iall,
    frows,
    frecv,
    fall,
    keys,
    w_sem,
    stage_sem,
    recv_sem,
    own_send,
    x_send,
    z_send,
    isem_s,
    isem_r,
    jsem_s,
    jsem_r,
    fsem_s,
    fsem_r,
    ksem_s,
    ksem_r,
    dsem,
):
    feats, toks = cot_ref.shape
    hidden = w_ref.shape[0]
    depth = feats // PIECES
    tiles = hidden // ROWS
    me = lax.axis_index("tensor")
    core = lax.axis_index("dp")
    z, x = me // 2, me % 2
    other = 1 - x
    o1 = z - 1 + 2 * ((3 - z) // 3)
    o3 = 3 * (1 - z // 2)
    o2 = 6 - z - o1 - o3
    across = {"tensor": z * 2 + other}
    peer = {"dp": 1 - core}

    order = [
        me,
        o1 * 2 + x,
        z * 2 + other,
        o2 * 2 + x,
        o1 * 2 + other,
        o3 * 2 + x,
        o2 * 2 + other,
        o3 * 2 + other,
    ]
    steps = [(shard, piece) for shard in range(8) for piece in range(PIECES)]

    def w_copy(step):
        index, piece = steps[step]
        start = pl.multiple_of(order[index] * feats + piece * depth, depth)
        return pltpu.make_async_copy(
            w_ref.at[:, pl.ds(start, depth)], wbuf.at[step % W_SLOTS], w_sem.at[step % W_SLOTS]
        )

    for step in range(W_SLOTS):
        w_copy(step).start()

    barrier = pltpu.get_barrier_semaphore()
    for shift in range(1, 8):
        pl.semaphore_signal(
            barrier, inc=1, device_id={"tensor": (me + shift) % 8}, device_id_type=MESH
        )
    pl.semaphore_signal(barrier, inc=1, device_id=peer, device_id_type=MESH)
    pl.semaphore_wait(barrier, 8)

    def remote(src, dst, send, recv, where):
        return pltpu.make_async_remote_copy(
            src_ref=src,
            dst_ref=dst,
            send_sem=send,
            recv_sem=recv,
            device_id=where,
            device_id_type=MESH,
        )

    def own_copy(piece, way):
        where = [
            across,
            {"tensor": jnp.minimum(me + 2, 6 + x)},
            {"tensor": jnp.maximum(me - 2, x)},
        ][way]
        return remote(
            cot_ref.at[pl.ds(piece * depth, depth)],
            held.at[me, pl.ds(piece * depth, depth)],
            own_send.at[way, piece],
            recv_sem.at[me, piece],
            where,
        )

    def x_copy(k, shard, piece):
        block = held.at[shard, pl.ds(piece * depth, depth)]
        return remote(block, block, x_send.at[k, piece], recv_sem.at[shard, piece], across)

    def z_copy(k, shard, piece, way):
        block = held.at[shard, pl.ds(piece * depth, depth)]
        return remote(
            block,
            block,
            z_send.at[k, piece],
            recv_sem.at[shard, piece],
            {"tensor": me + 2 * way},
        )

    def z_forward(k, piece, act):
        source = [o1, o2, o3][k]

        @pl.when(jnp.logical_and(source < z, z < 3))
        def _():
            act(z_copy(k, source * 2 + x, piece, 1))

        @pl.when(jnp.logical_and(source > z, z > 0))
        def _():
            act(z_copy(k, source * 2 + x, piece, -1))

    def own_moves(act):
        for piece in range(PIECES):
            act(own_copy(piece, 0))

            @pl.when(z < 3)
            def _():
                act(own_copy(piece, 1))

            @pl.when(z > 0)
            def _():
                act(own_copy(piece, 2))

    own_moves(lambda copy: copy.start())

    def i_copy(shift):
        to = (me + shift) % 8
        return remote(
            inp_ref.at[pl.ds(pl.multiple_of(to * 8, 8), 8)],
            irecv.at[shift - 1],
            isem_s.at[shift - 1],
            isem_r.at[shift - 1],
            {"tensor": to},
        )

    for shift in range(1, 8):
        i_copy(shift).start()

    def stage_copy(which, tile, slot):
        ref = [gate_ref, up_ref][which]
        return pltpu.make_async_copy(
            ref.at[pl.ds(pl.multiple_of(tile * ROWS, ROWS), ROWS)],
            stage.at[which, slot],
            stage_sem.at[which, slot],
        )

    for which in range(2):
        stage_copy(which, 0, 0).start()

    def multiply(step, first=False):
        index, piece = steps[step]
        block = cot_ref if index == 0 else held.at[order[index]]
        w_copy(step).wait()

        @pl.loop(0, tiles)
        def _(tile):
            rows = pl.ds(pl.multiple_of(tile * ROWS, ROWS), ROWS)
            part = jnp.dot(
                wbuf[step % W_SLOTS, rows, :],
                block[pl.ds(piece * depth, depth), :],
                preferred_element_type=F32,
            )
            if first:
                acc[rows, :] = part
            else:
                acc[rows, :] += part

        if step + W_SLOTS < len(steps):
            w_copy(step + W_SLOTS).start()

    for piece in range(PIECES):
        multiply(piece, first=piece == 0)

    for tile in range(tiles):
        slot = tile % 2
        for which in range(2):
            if tile + 1 < tiles:
                stage_copy(which, tile + 1, 1 - slot).start()
            stage_copy(which, tile, slot).wait()

        @pl.loop(0, ROWS // 64)
        def _(part):
            rows = pl.ds(pl.multiple_of(part * 64, 64), 64)
            target = pl.ds(pl.multiple_of(tile * ROWS + part * 64, 64), 64)
            activated, slope = silu_parts(stage[0, slot, rows, :].astype(F32))
            gate_mul[target, :] = stage[1, slot, rows, :].astype(F32) * slope
            up_mul[target, :] = activated

    for shift in range(1, 8):
        i_copy(shift).wait_recv()
    my_rows = pl.ds(pl.multiple_of(me * 8, 8), 8)
    total = inp_ref[my_rows, :]
    for shift in range(1, 8):
        total = total + irecv[shift - 1]
    iall[core, my_rows, :] = total

    def j_copy(shift):
        block = iall.at[core, my_rows]
        return remote(
            block,
            block,
            jsem_s.at[shift - 1],
            jsem_r.at[shift - 1],
            {"tensor": (me + shift) % 8},
        )

    for shift in range(1, 8):
        j_copy(shift).start()

    for index in range(1, 8):
        if index == 4:
            for shift in range(1, 8):
                j_copy(shift).wait_recv()
            i_swap = remote(iall.at[core], iall.at[core], dsem.at[0], dsem.at[1], peer)
            i_swap.start()
        for piece in range(PIECES):
            shard = order[index]
            block = held.at[shard, pl.ds(piece * depth, depth)]
            remote(
                block, block, own_send.at[0, piece], recv_sem.at[shard, piece], across
            ).wait_recv()
            if index in (1, 3, 5):
                k = index // 2
                z_forward(k, piece, lambda copy: copy.start())
                x_copy(k, shard, piece).start()
            multiply(index * PIECES + piece)

    rank = pg_ref.shape[1]
    frows[...] = jnp.zeros_like(frows)

    @pl.loop(0, tiles)
    def _(tile):
        rows = pl.ds(pl.multiple_of(tile * ROWS, ROWS), ROWS)
        grad = acc[rows, :]
        gate_grad = (grad * gate_mul[rows, :]).astype(BF16)
        up_grad = (grad * up_mul[rows, :]).astype(BF16)
        frows[pl.ds(0, rank), :] += contract_first(pg_ref[rows, :], gate_grad)
        frows[pl.ds(rank, rank), :] += contract_first(pu_ref[rows, :], up_grad)

    def f_copy(shift):
        to = (me + shift) % 8
        return remote(
            frows.at[pl.ds(pl.multiple_of(to * 16, 16), 16)],
            frecv.at[shift - 1],
            fsem_s.at[shift - 1],
            fsem_r.at[shift - 1],
            {"tensor": to},
        )

    for shift in range(1, 8):
        f_copy(shift).start()
    summed = frows[pl.ds(pl.multiple_of(me * 16, 16), 16), :]
    for shift in range(1, 8):
        f_copy(shift).wait_recv()
        summed = summed + frecv[shift - 1]
    fall[core] = summed
    f_swap = remote(fall.at[core], fall.at[core], dsem.at[2], dsem.at[3], peer)
    f_swap.start()
    i_swap.wait()
    f_swap.wait()

    slots = mask_ref.shape[0]
    for slot in range(slots):
        value = jnp.zeros((16, rank), F32)
        for d in range(2):
            value = value + contract_last(
                fall[d] * mask_ref[pl.ds(slot, 1), pl.ds(d * toks, toks)], iall[d]
            )
        keys[me, pl.ds(slot * 16, 16), :] = value.astype(BF16)

    def k_copy(shift):
        block = keys.at[me]
        return remote(
            block,
            block,
            ksem_s.at[shift - 1],
            ksem_r.at[shift - 1],
            {"tensor": (me + shift) % 8},
        )

    for shift in range(1, 8):
        k_copy(shift).start()
    for shift in range(1, 8):
        k_copy(shift).wait_recv()
    out_ref[...] = keys[...]

    own_moves(lambda copy: copy.wait_send())
    for k, source in enumerate((o1, o2, o3)):
        for piece in range(PIECES):
            z_forward(k, piece, lambda copy: copy.wait_send())
            x_copy(k, source * 2 + x, piece).wait_send()
    for shift in range(1, 8):
        i_copy(shift).wait_send()
        j_copy(shift).wait_send()
        f_copy(shift).wait_send()
        k_copy(shift).wait_send()


def fused_keys(cotangent, down_weight, gate_pre, up_pre, proj_gate, proj_up, partial, mask):
    feats, toks = cotangent.shape
    hidden, width = down_weight.shape
    rank = proj_gate.shape[1]
    slots = mask.shape[0]
    vmem = pl.BlockSpec(memory_space=pltpu.VMEM)
    hbm = pl.BlockSpec(memory_space=pl.ANY)
    sems = pltpu.SemaphoreType.DMA
    return pl.pallas_call(
        keys_kernel,
        out_shape=jax.ShapeDtypeStruct((8, slots * 16, rank), BF16),
        in_specs=[vmem, hbm, hbm, hbm, vmem, vmem, vmem, vmem],
        out_specs=vmem,
        scratch_shapes=[
            pltpu.VMEM((8, feats, toks), BF16),
            pltpu.VMEM((W_SLOTS, hidden, feats // PIECES), BF16),
            pltpu.VMEM((hidden, toks), F32),
            pltpu.VMEM((hidden, toks), F32),
            pltpu.VMEM((hidden, toks), F32),
            pltpu.VMEM((2, 2, ROWS, toks), BF16),
            pltpu.VMEM((7, 8, toks), F32),
            pltpu.VMEM((2, rank, toks), F32),
            pltpu.VMEM((2 * rank, toks), F32),
            pltpu.VMEM((7, 16, toks), F32),
            pltpu.VMEM((2, 16, toks), F32),
            pltpu.VMEM((8, slots * 16, rank), BF16),
            sems((W_SLOTS,)),
            sems((2, 2)),
            sems((8, PIECES)),
            sems((3, PIECES)),
            sems((3, PIECES)),
            sems((3, PIECES)),
            sems((7,)),
            sems((7,)),
            sems((7,)),
            sems((7,)),
            sems((7,)),
            sems((7,)),
            sems((7,)),
            sems((7,)),
            sems((4,)),
        ],
        compiler_params=pltpu.CompilerParams(
            collective_id=0, has_side_effects=True, vmem_limit_bytes=60 * 2**20
        ),
        cost_estimate=pl.CostEstimate(
            flops=2 * hidden * width * toks,
            bytes_accessed=2 * hidden * (width + 2 * toks),
            transcendentals=hidden * toks,
        ),
    )(cotangent, down_weight, gate_pre, up_pre, proj_gate, proj_up, partial, mask)


def per_device_fused(
    cotangent,
    layer_input,
    gate_pre,
    up_pre,
    down_weight,
    proj_input,
    proj_gate,
    proj_up,
    store_slot,
    example_ids,
    lengths,
):
    toks = cotangent.shape[1]
    rank = proj_gate.shape[1]
    seqs = lengths.shape[0]
    seq_len = toks // seqs
    core = lax.axis_index("dp")
    mine = jnp.stack([store_slot, example_ids, lengths])
    theirs = lax.ppermute(mine, "dp", [(0, 1), (1, 0)])
    first = jnp.where(core == 0, mine, theirs)
    second = jnp.where(core == 0, theirs, mine)
    slot_all, id_all, len_all = jnp.concatenate([first, second], axis=1)
    wanted = core * seqs + jnp.arange(seqs, dtype=jnp.int32)
    chosen = slot_all[None, :] == wanted[:, None]
    position = jnp.arange(seq_len, dtype=jnp.int32)
    inside = jnp.where(position[None, :] < len_all[:, None], 1.0, 0.0).astype(F32)
    weight = inside * lax.rsqrt(len_all.astype(F32))[:, None]
    mask = jnp.where(chosen[:, :, None], weight[None], 0.0).reshape(seqs, 2 * toks)
    store_ids = jnp.sum(jnp.where(chosen, id_all[None, :], 0), axis=1).astype(jnp.int32)
    partial = contract_first(proj_input, layer_input)
    keys = fused_keys(
        cotangent, down_weight, gate_pre, up_pre, proj_gate, proj_up, partial, mask
    )
    keys = keys.reshape(8, seqs, 16, rank).transpose(1, 0, 2, 3)
    return (keys.reshape(seqs, 2 * rank * rank), store_ids)


def per_device_plain(
    cotangent,
    layer_input,
    gate_pre,
    up_pre,
    down_weight,
    proj_input,
    proj_gate,
    proj_up,
    store_slot,
    example_ids,
    lengths,
):
    tok_count = cotangent.shape[1]
    proj_rank = proj_gate.shape[1]
    seq_count = lengths.shape[0]
    seq_len = tok_count // seq_count
    hidden_grad = jnp.dot(
        down_weight,
        lax.all_gather(cotangent, "tensor", axis=0, tiled=True),
        preferred_element_type=jnp.float32,
    )
    input_partial = contract_first(proj_input, layer_input)
    gate_value = gate_pre.astype(jnp.float32)
    up_value = up_pre.astype(jnp.float32)
    activated, slope = silu_parts(gate_value)
    gate_grad = (hidden_grad * up_value * slope).astype(jnp.bfloat16)
    up_grad = (hidden_grad * activated).astype(jnp.bfloat16)
    gate_factor = contract_first(proj_gate, gate_grad)
    up_factor = contract_first(proj_up, up_grad)
    partial_rows = jnp.concatenate([gate_factor, up_factor, input_partial], axis=0)
    inverse_root = lax.rsqrt(lengths.astype(jnp.float32))
    summed = lax.psum(partial_rows, "tensor")
    input_factor = summed[2 * proj_rank :]
    position = jnp.arange(seq_len, dtype=jnp.int32)
    inside = jnp.where(position[None, :] < lengths[:, None], 1.0, 0.0).astype(jnp.float32)
    weight = inside * inverse_root[:, None]
    grads_three = summed[: 2 * proj_rank].reshape(2, proj_rank, seq_count, seq_len)
    inputs_three = input_factor.reshape(proj_rank, seq_count, seq_len)
    key_values = jnp.einsum(
        "gael,bel,el->egab", grads_three, inputs_three, weight, precision=lax.Precision.HIGHEST
    )
    key_values = key_values.reshape(seq_count, -1)
    key_rows = key_values.astype(jnp.bfloat16)
    dp_count = lax.axis_size("dp")
    slot_index = jnp.arange(dp_count * seq_count, dtype=jnp.int32)
    chosen = store_slot[None, :] == slot_index[:, None]
    outgoing = jnp.dot(
        chosen.astype(jnp.bfloat16), key_rows, preferred_element_type=jnp.float32
    ).astype(jnp.bfloat16)
    outgoing = outgoing.reshape(dp_count, seq_count, -1)
    outgoing_ids = jnp.sum(jnp.where(chosen, example_ids[None, :], 0), axis=1).reshape(
        dp_count, seq_count
    )
    arrived, arrived_ids = (
        lax.all_to_all(outgoing, "dp", split_axis=0, concat_axis=0, tiled=True),
        lax.all_to_all(outgoing_ids, "dp", split_axis=0, concat_axis=0, tiled=True),
    )
    store_keys = jnp.sum(arrived.astype(jnp.float32), axis=0).astype(jnp.bfloat16)
    store_ids = jnp.sum(arrived_ids, axis=0).astype(jnp.int32)
    return (store_keys, store_ids)


def solution(mesh):
    placed = (
        P("tensor", ("parts", "dp")),
        P("tensor", ("parts", "dp")),
        P("tensor", ("parts", "dp")),
        P("tensor", ("parts", "dp")),
        P("tensor", None),
        P("tensor", None),
        P("tensor", None),
        P("tensor", None),
        P(("parts", "dp")),
        P(("parts", "dp")),
        P(("parts", "dp")),
    )
    fits = mesh.shape["tensor"] == 8 and mesh.shape["dp"] == 2
    return jax.shard_map(
        per_device_fused if fits else per_device_plain,
        mesh=mesh,
        in_specs=placed,
        out_specs=(P(("parts", "dp"), None), P(("parts", "dp"))),
        check_vma=False,
    )
```

```python
import functools

import jax
import jax.numpy as jnp
from jax import lax
from jax.experimental import pallas as pl
from jax.experimental.pallas import tpu as pltpu
from jax.sharding import PartitionSpec as P

MESH = pl.DeviceIdType.MESH
F32 = jnp.float32
BF16 = jnp.bfloat16
PIECES = 4
PAIRS = 2
W_SLOTS = 3
ROWS = 512
PART = 256


def silu_parts(gate_value):
    sigmoid_gate = jax.nn.sigmoid(gate_value)
    return (gate_value * sigmoid_gate, sigmoid_gate * (1.0 + gate_value * (1.0 - sigmoid_gate)))


def contract_first(left, right):
    return lax.dot_general(
        left, right, (((0,), (0,)), ((), ())), preferred_element_type=jnp.float32
    )


def dot(left, right):
    return jnp.dot(left, right, preferred_element_type=jnp.float32)


def dot_exact(left, right):
    return jnp.dot(
        left, right, precision=lax.Precision.HIGHEST, preferred_element_type=jnp.float32
    )


def contract_last(left, right):
    return lax.dot_general(
        left,
        right,
        (((1,), (1,)), ((), ())),
        precision=lax.Precision.HIGHEST,
        preferred_element_type=jnp.float32,
    )


def keys_kernel(
    mine_ref,
    theirs_ref,
    cot_ref,
    lin_hbm,
    w_ref,
    gate_ref,
    up_ref,
    pi_hbm,
    pg_hbm,
    pu_hbm,
    out_ref,
    perm,
    mask,
    spare,
    packed,
    gate_up_spare,
    lin,
    pi,
    pg,
    pu,
    inp,
    held,
    wbuf,
    acc,
    gate_mul,
    up_mul,
    stage,
    irecv,
    iall,
    ipacked,
    frows,
    frecv,
    fall,
    keys,
    w_sem,
    stage_sem,
    load_sem,
    recv_sem,
    own_send,
    x_send,
    z_send,
    extra_send,
    isem_s,
    isem_r,
    jsem_s,
    jsem_r,
    fsem_s,
    fsem_r,
    ksem_s,
    ksem_r,
    dsem_s,
    dsem_r,
):
    feats, slots_all = cot_ref.shape
    hidden = w_ref.shape[0]
    toks = packed.shape[1]
    seqs = mine_ref.shape[1]
    length = slots_all // seqs
    rank = pg.shape[0]
    depth = feats // PIECES
    wide = feats // PAIRS
    per_pair = PIECES // PAIRS
    tiles = hidden // ROWS
    me = lax.axis_index("tensor")
    core = lax.axis_index("dp")
    z, x = me // 2, me % 2
    other = 1 - x
    o1 = z - 1 + 2 * ((3 - z) // 3)
    o3 = 3 * (1 - z // 2)
    o2 = 6 - z - o1 - o3
    across = {"tensor": z * 2 + other}
    peer = {"dp": 1 - core}

    order = [
        me,
        o1 * 2 + x,
        z * 2 + other,
        o2 * 2 + x,
        o1 * 2 + other,
        o3 * 2 + x,
        o2 * 2 + other,
        o3 * 2 + other,
    ]
    steps = [(shard, pair) for shard in range(8) for pair in range(PAIRS)]

    def w_copy(step):
        index, pair = steps[step]
        start = pl.multiple_of(order[index] * feats + pair * wide, wide)
        return pltpu.make_async_copy(
            w_ref.at[:, pl.ds(start, wide)], wbuf.at[step % W_SLOTS], w_sem.at[step % W_SLOTS]
        )

    loads = [
        pltpu.make_async_copy(source, target, load_sem.at[i])
        for i, (source, target) in enumerate(
            ((lin_hbm, lin), (pi_hbm, pi), (pg_hbm, pg), (pu_hbm, pu))
        )
    ]

    def stage_copy(which, tile):
        ref = [gate_ref, up_ref][which]
        return pltpu.make_async_copy(
            ref.at[pl.ds(tile * ROWS, ROWS)], stage.at[which, tile % 2], stage_sem.at[which, tile % 2]
        )

    loads[0].start()
    loads[1].start()
    for step in range(W_SLOTS):
        w_copy(step).start()
    loads[2].start()
    loads[3].start()
    for which in range(2):
        stage_copy(which, 0).start()

    barrier = pltpu.get_barrier_semaphore()
    for shift in range(1, 8):
        pl.semaphore_signal(
            barrier, inc=1, device_id={"tensor": (me + shift) % 8}, device_id_type=MESH
        )
    pl.semaphore_signal(barrier, inc=1, device_id=peer, device_id_type=MESH)

    def remote(src, dst, send, recv, where):
        return pltpu.make_async_remote_copy(
            src_ref=src,
            dst_ref=dst,
            send_sem=send,
            recv_sem=recv,
            device_id=where,
            device_id_type=MESH,
        )

    def lengths_of(ref):
        return [ref[2, s] for s in range(seqs)]

    def plan(ref):
        long = lengths_of(ref)
        count = sum(long[1:], long[0])
        spill = jnp.maximum(count - toks, 0)
        kept = long[:-1] + [long[-1] - spill]
        starts = [jnp.int32(0)]
        for value in long[:-1]:
            starts.append(starts[-1] + value)
        return long, count, spill, kept, starts

    def make_perm(view, own, far):
        long, count, spill, kept, starts = plan(own)
        far_long, _, far_spill, far_kept, _ = plan(far)
        row = lax.broadcasted_iota(jnp.int32, (length, toks), 0)
        gap = lax.broadcasted_iota(jnp.int32, (length, toks), 1) - row
        for s in range(seqs):
            hit = jnp.logical_and(gap == starts[s], row < kept[s])
            perm[view, pl.ds(s * length, length), :] = jnp.where(hit, 1.0, 0.0).astype(BF16)
        hit = jnp.logical_and(
            gap == count - far_kept[-1],
            jnp.logical_and(row >= far_kept[-1], row < far_long[-1]),
        )
        perm[view, pl.ds(slots_all, length), :] = jnp.where(hit, 1.0, 0.0).astype(BF16)

    def make_mask(view, own, far):
        long, count, spill, kept, starts = plan(own)
        far_long, _, far_spill, _, _ = plan(far)
        column = lax.broadcasted_iota(jnp.int32, (seqs, toks), 1)
        wanted = lax.broadcasted_iota(jnp.int32, (seqs, toks), 0) + core * seqs
        entries = [
            (starts[s], kept[s], long[s], own[0, s]) for s in range(seqs)
        ] + [(count, far_spill, far_long[-1], far[0, seqs - 1])]
        value = jnp.zeros((seqs, toks), F32)
        for first, many, full, slot in entries:
            hit = jnp.logical_and(column >= first, column < first + many)
            hit = jnp.logical_and(hit, wanted == slot)
            scale = lax.rsqrt(jnp.full((seqs, toks), full, jnp.int32).astype(F32))
            value = value + jnp.where(hit, scale, 0.0)
        mask[view] = value

    last = pl.ds(slots_all - length, length)
    make_perm(0, mine_ref, theirs_ref)
    pl.semaphore_wait(barrier, 8)

    c_swap = remote(cot_ref.at[:, last], spare, dsem_s.at[0], dsem_r.at[0], peer)
    c_swap.start()
    g_swaps = [
        remote(ref.at[:, last], gate_up_spare.at[i], dsem_s.at[1 + i], dsem_r.at[1 + i], peer)
        for i, ref in enumerate((gate_ref, up_ref))
    ]

    def own_copy(piece, way):
        where = [
            across,
            {"tensor": jnp.minimum(me + 2, 6 + x)},
            {"tensor": jnp.maximum(me - 2, x)},
        ][way]
        return remote(
            packed.at[pl.ds(piece * depth, depth)],
            held.at[me, pl.ds(piece * depth, depth)],
            own_send.at[way, piece],
            recv_sem.at[me, piece],
            where,
        )

    def block_copy(shard, piece, send, where):
        block = held.at[shard, pl.ds(piece * depth, depth)]
        return remote(block, block, send, recv_sem.at[shard, piece], where)

    def x_copy(k, shard, piece):
        return block_copy(shard, piece, x_send.at[k, piece], across)

    def z_forward(k, piece, act):
        source = [o1, o2, o3][k]
        for way, holds in (
            (1, jnp.logical_and(source < z, z < 3)),
            (-1, jnp.logical_and(source > z, z > 0)),
        ):

            @pl.when(holds)
            def _():
                act(
                    block_copy(
                        source * 2 + x, piece, z_send.at[k, piece], {"tensor": me + 2 * way}
                    )
                )

    def extra_forward(piece, act):
        for i, (way, holds) in enumerate(((1, z < 3), (-1, z == 1))):

            @pl.when(holds)
            def _():
                act(
                    block_copy(
                        z * 2 + other, piece, extra_send.at[i, piece], {"tensor": me + 2 * way}
                    )
                )

    def own_moves(piece, act):
        act(own_copy(piece, 0))

        @pl.when(z < 3)
        def _():
            act(own_copy(piece, 1))

        @pl.when(z > 0)
        def _():
            act(own_copy(piece, 2))

    def start(copy):
        copy.start()

    def wait_send(copy):
        copy.wait_send()

    c_swap.wait_recv()
    for piece in range(PIECES):
        rows = pl.ds(piece * depth, depth)
        packed[rows, :] = (
            dot(cot_ref[rows, :], perm[0, pl.ds(0, slots_all), :])
            + dot(spare[rows, :], perm[0, pl.ds(slots_all, length), :])
        ).astype(BF16)
        own_moves(piece, start)
    for swap in g_swaps:
        swap.start()

    loads[0].wait()
    loads[1].wait()
    inp[...] = dot(pi[...], lin[...])

    def i_copy(shift):
        to = (me + shift) % 8
        return remote(
            inp.at[pl.ds(pl.multiple_of(to * 8, 8), 8)],
            irecv.at[shift - 1],
            isem_s.at[shift - 1],
            isem_r.at[shift - 1],
            {"tensor": to},
        )

    for shift in range(1, 8):
        i_copy(shift).start()

    def multiply(step, first=False):
        index, pair = steps[step]
        block = packed if index == 0 else held.at[order[index]]
        w_copy(step).wait()

        @pl.loop(0, tiles)
        def _(tile):
            rows = pl.ds(pl.multiple_of(tile * ROWS, ROWS), ROWS)
            part = dot(wbuf[step % W_SLOTS, rows, :], block[pl.ds(pair * wide, wide), :])
            if first:
                acc[rows, :] = part
            else:
                acc[rows, :] += part

        if step + W_SLOTS < len(steps):
            w_copy(step + W_SLOTS).start()

    def slopes(tile):
        slot = tile % 2
        for which in range(2):
            if tile + 1 < tiles:
                stage_copy(which, tile + 1).start()
            stage_copy(which, tile).wait()

        @pl.loop(0, ROWS // PART)
        def _(part):
            rows = pl.ds(pl.multiple_of(part * PART, PART), PART)
            target = pl.ds(pl.multiple_of(tile * ROWS + part * PART, PART), PART)
            gate_value, up_value = [
                dot(stage[which, slot, rows, :], perm[0, pl.ds(0, slots_all), :])
                + dot(gate_up_spare[which, target, :], perm[0, pl.ds(slots_all, length), :])
                for which in range(2)
            ]
            activated, slope = silu_parts(gate_value)
            gate_mul[target, :] = up_value * slope
            up_mul[target, :] = activated

    for pair in range(PAIRS):
        multiply(pair, first=pair == 0)
    for swap in g_swaps:
        swap.wait_recv()
    for tile in range(3):
        slopes(tile)

    my_rows = pl.ds(pl.multiple_of(me * 8, 8), 8)

    def j_copy(shift):
        block = iall.at[core, my_rows]
        return remote(
            block,
            block,
            jsem_s.at[shift - 1],
            jsem_r.at[shift - 1],
            {"tensor": (me + shift) % 8},
        )

    for index in range(1, 8):
        if index == 3:
            for shift in range(1, 8):
                i_copy(shift).wait_recv()
            total = inp[my_rows, :]
            for shift in range(1, 8):
                total = total + irecv[shift - 1]
            iall[core, my_rows, :] = total
            for shift in range(1, 8):
                j_copy(shift).start()
            make_perm(1, theirs_ref, mine_ref)
            make_mask(0, mine_ref, theirs_ref)
            make_mask(1, theirs_ref, mine_ref)
        if index == 4:
            for shift in range(1, 8):
                j_copy(shift).wait_recv()
            i_swap = remote(iall.at[core], iall.at[core], dsem_s.at[3], dsem_r.at[3], peer)
            i_swap.start()
        if index == 6:
            i_swap.wait_recv()
            for view, near in ((0, core), (1, 1 - core)):
                ipacked[view] = dot_exact(
                    iall[near], perm[view, pl.ds(0, slots_all), :].astype(F32)
                ) + dot_exact(
                    iall[1 - near, :, pl.ds(slots_all - length, length)],
                    perm[view, pl.ds(slots_all, length), :].astype(F32),
                )
        shard = order[index]
        for pair in range(PAIRS):
            for piece in range(pair * per_pair, (pair + 1) * per_pair):
                block_copy(shard, piece, own_send.at[0, piece], across).wait_recv()
                if index in (1, 3, 5):
                    k = index // 2
                    z_forward(k, piece, start)
                    if k > 0 or piece < PIECES // 2:
                        x_copy(k, shard, piece).start()
                if index == 2 and piece >= PIECES // 2:
                    extra_forward(piece, start)
            multiply(index * PAIRS + pair)
        if index <= 2:
            slopes(1 + 2 * index)
            slopes(2 + 2 * index)

    loads[2].wait()
    loads[3].wait()
    gate_sum = jnp.zeros((rank, toks), F32)
    up_sum = jnp.zeros((rank, toks), F32)
    for tile in range(tiles):
        rows = pl.ds(tile * ROWS, ROWS)
        grad = acc[rows, :]
        gate_grad = (grad * gate_mul[rows, :]).astype(BF16)
        up_grad = (grad * up_mul[rows, :]).astype(BF16)
        gate_sum = gate_sum + dot(pg[:, rows], gate_grad)
        up_sum = up_sum + dot(pu[:, rows], up_grad)
    frows[pl.ds(0, rank), :] = gate_sum
    frows[pl.ds(rank, rank), :] = up_sum

    def f_copy(shift):
        to = (me + shift) % 8
        return remote(
            frows.at[pl.ds(pl.multiple_of(to * 16, 16), 16)],
            frecv.at[shift - 1],
            fsem_s.at[shift - 1],
            fsem_r.at[shift - 1],
            {"tensor": to},
        )

    for shift in range(1, 8):
        f_copy(shift).start()
    summed = frows[pl.ds(pl.multiple_of(me * 16, 16), 16), :]
    for shift in range(1, 8):
        f_copy(shift).wait_recv()
        summed = summed + frecv[shift - 1]
    fall[core] = summed
    f_swap = remote(fall.at[core], fall.at[core], dsem_s.at[4], dsem_r.at[4], peer)
    f_swap.start()
    f_swap.wait_recv()

    for s in range(seqs):
        value = jnp.zeros((16, rank), F32)
        for view, near in ((0, core), (1, 1 - core)):
            value = value + contract_last(
                fall[near] * mask[view, pl.ds(s, 1), :], ipacked[view]
            )
        keys[me, pl.ds(s * 16, 16), :] = value.astype(BF16)

    def k_copy(shift):
        block = keys.at[me]
        return remote(
            block,
            block,
            ksem_s.at[shift - 1],
            ksem_r.at[shift - 1],
            {"tensor": (me + shift) % 8},
        )

    for shift in range(1, 8):
        k_copy(shift).start()

    for swap in [c_swap, i_swap, f_swap] + g_swaps:
        swap.wait_send()
    for piece in range(PIECES):
        own_moves(piece, wait_send)
        if piece >= PIECES // 2:
            extra_forward(piece, wait_send)
        for k, source in enumerate((o1, o2, o3)):
            z_forward(k, piece, wait_send)
            if k > 0 or piece < PIECES // 2:
                x_copy(k, source * 2 + x, piece).wait_send()
    for shift in range(1, 8):
        i_copy(shift).wait_send()
        j_copy(shift).wait_send()
        f_copy(shift).wait_send()

    for shift in range(1, 8):
        k_copy(shift).wait_recv()
    for t in range(8):
        for s in range(seqs):
            out_ref[s, pl.ds(t * 16, 16), :] = keys[t, pl.ds(s * 16, 16), :]
    for shift in range(1, 8):
        k_copy(shift).wait_send()


def fused_keys(mine, theirs, cotangent, layer_input, down_weight, gate_pre, up_pre, pi, pg, pu):
    feats, slots_all = cotangent.shape
    hidden, width = down_weight.shape
    rank = pg.shape[0]
    seqs = mine.shape[1]
    length = slots_all // seqs
    toks = slots_all - length
    smem = pl.BlockSpec(memory_space=pltpu.SMEM)
    vmem = pl.BlockSpec(memory_space=pltpu.VMEM)
    hbm = pl.BlockSpec(memory_space=pl.ANY)
    sems = pltpu.SemaphoreType.DMA
    return pl.pallas_call(
        keys_kernel,
        out_shape=jax.ShapeDtypeStruct((seqs, 2 * rank, rank), BF16),
        in_specs=[smem, smem, vmem] + [hbm] * 7,
        out_specs=vmem,
        scratch_shapes=[
            pltpu.VMEM((2, slots_all + length, toks), BF16),
            pltpu.VMEM((2, seqs, toks), F32),
            pltpu.VMEM((feats, length), BF16),
            pltpu.VMEM((feats, toks), BF16),
            pltpu.VMEM((2, hidden, length), BF16),
            pltpu.VMEM((feats, slots_all), BF16),
            pltpu.VMEM((rank, feats), BF16),
            pltpu.VMEM((rank, hidden), BF16),
            pltpu.VMEM((rank, hidden), BF16),
            pltpu.VMEM((rank, slots_all), F32),
            pltpu.VMEM((8, feats, toks), BF16),
            pltpu.VMEM((W_SLOTS, hidden, feats // PAIRS), BF16),
            pltpu.VMEM((hidden, toks), F32),
            pltpu.VMEM((hidden, toks), F32),
            pltpu.VMEM((hidden, toks), F32),
            pltpu.VMEM((2, 2, ROWS, slots_all), BF16),
            pltpu.VMEM((7, 8, slots_all), F32),
            pltpu.VMEM((2, rank, slots_all), F32),
            pltpu.VMEM((2, rank, toks), F32),
            pltpu.VMEM((2 * rank, toks), F32),
            pltpu.VMEM((7, 16, toks), F32),
            pltpu.VMEM((2, 16, toks), F32),
            pltpu.VMEM((8, seqs * 16, rank), BF16),
            sems((W_SLOTS,)),
            sems((2, 2)),
            sems((4,)),
            sems((8, PIECES)),
            sems((3, PIECES)),
            sems((3, PIECES)),
            sems((3, PIECES)),
            sems((2, PIECES)),
        ]
        + [sems((7,))] * 8
        + [sems((5,))] * 2,
        compiler_params=pltpu.CompilerParams(
            collective_id=0, has_side_effects=True, vmem_limit_bytes=60 * 2**20
        ),
        cost_estimate=pl.CostEstimate(
            flops=2 * hidden * width * toks,
            bytes_accessed=2 * hidden * (width + 2 * slots_all),
            transcendentals=hidden * toks,
        ),
    )(mine, theirs, cotangent, layer_input, down_weight, gate_pre, up_pre, pi, pg, pu)


def per_device_fused(
    cotangent,
    layer_input,
    gate_pre,
    up_pre,
    down_weight,
    proj_input,
    proj_gate,
    proj_up,
    store_slot,
    example_ids,
    lengths,
):
    rank = proj_gate.shape[1]
    seqs = lengths.shape[0]
    core = lax.axis_index("dp")
    mine = jnp.stack([store_slot, example_ids, lengths])
    theirs = lax.ppermute(mine, "dp", [(0, 1), (1, 0)])
    wanted = core * seqs + jnp.arange(seqs, dtype=jnp.int32)
    both = jnp.concatenate([mine, theirs], axis=1)
    chosen = both[0][None, :] == wanted[:, None]
    store_ids = jnp.sum(jnp.where(chosen, both[1][None, :], 0), axis=1).astype(jnp.int32)
    keys = fused_keys(
        mine,
        theirs,
        cotangent,
        layer_input,
        down_weight,
        gate_pre,
        up_pre,
        proj_input.T,
        proj_gate.T,
        proj_up.T,
    )
    return (keys.reshape(seqs, 2 * rank * rank), store_ids)


def per_device_plain(
    cotangent,
    layer_input,
    gate_pre,
    up_pre,
    down_weight,
    proj_input,
    proj_gate,
    proj_up,
    store_slot,
    example_ids,
    lengths,
):
    tok_count = cotangent.shape[1]
    proj_rank = proj_gate.shape[1]
    seq_count = lengths.shape[0]
    seq_len = tok_count // seq_count
    hidden_grad = jnp.dot(
        down_weight,
        lax.all_gather(cotangent, "tensor", axis=0, tiled=True),
        preferred_element_type=jnp.float32,
    )
    input_partial = contract_first(proj_input, layer_input)
    gate_value = gate_pre.astype(jnp.float32)
    up_value = up_pre.astype(jnp.float32)
    activated, slope = silu_parts(gate_value)
    gate_grad = (hidden_grad * up_value * slope).astype(jnp.bfloat16)
    up_grad = (hidden_grad * activated).astype(jnp.bfloat16)
    gate_factor = contract_first(proj_gate, gate_grad)
    up_factor = contract_first(proj_up, up_grad)
    partial_rows = jnp.concatenate([gate_factor, up_factor, input_partial], axis=0)
    inverse_root = lax.rsqrt(lengths.astype(jnp.float32))
    summed = lax.psum(partial_rows, "tensor")
    input_factor = summed[2 * proj_rank :]
    position = jnp.arange(seq_len, dtype=jnp.int32)
    inside = jnp.where(position[None, :] < lengths[:, None], 1.0, 0.0).astype(jnp.float32)
    weight = inside * inverse_root[:, None]
    grads_three = summed[: 2 * proj_rank].reshape(2, proj_rank, seq_count, seq_len)
    inputs_three = input_factor.reshape(proj_rank, seq_count, seq_len)
    key_values = jnp.einsum(
        "gael,bel,el->egab", grads_three, inputs_three, weight, precision=lax.Precision.HIGHEST
    )
    key_values = key_values.reshape(seq_count, -1)
    key_rows = key_values.astype(jnp.bfloat16)
    dp_count = lax.axis_size("dp")
    slot_index = jnp.arange(dp_count * seq_count, dtype=jnp.int32)
    chosen = store_slot[None, :] == slot_index[:, None]
    outgoing = jnp.dot(
        chosen.astype(jnp.bfloat16), key_rows, preferred_element_type=jnp.float32
    ).astype(jnp.bfloat16)
    outgoing = outgoing.reshape(dp_count, seq_count, -1)
    outgoing_ids = jnp.sum(jnp.where(chosen, example_ids[None, :], 0), axis=1).reshape(
        dp_count, seq_count
    )
    arrived, arrived_ids = (
        lax.all_to_all(outgoing, "dp", split_axis=0, concat_axis=0, tiled=True),
        lax.all_to_all(outgoing_ids, "dp", split_axis=0, concat_axis=0, tiled=True),
    )
    store_keys = jnp.sum(arrived.astype(jnp.float32), axis=0).astype(jnp.bfloat16)
    store_ids = jnp.sum(arrived_ids, axis=0).astype(jnp.int32)
    return (store_keys, store_ids)


def solution(mesh):
    placed = (
        P("tensor", ("parts", "dp")),
        P("tensor", ("parts", "dp")),
        P("tensor", ("parts", "dp")),
        P("tensor", ("parts", "dp")),
        P("tensor", None),
        P("tensor", None),
        P("tensor", None),
        P("tensor", None),
        P(("parts", "dp")),
        P(("parts", "dp")),
        P(("parts", "dp")),
    )
    fits = mesh.shape["tensor"] == 8 and mesh.shape["dp"] == 2
    return jax.shard_map(
        per_device_fused if fits else per_device_plain,
        mesh=mesh,
        in_specs=placed,
        out_specs=(P(("parts", "dp"), None), P(("parts", "dp"))),
        check_vma=False,
    )
```

```python
import functools

import jax
import jax.numpy as jnp
from jax import lax
from jax.experimental import pallas as pl
from jax.experimental.pallas import tpu as pltpu
from jax.sharding import PartitionSpec as P

MESH = pl.DeviceIdType.MESH
F32 = jnp.float32
BF16 = jnp.bfloat16
PIECES = 4
PAIRS = 2
W_SLOTS = 3
ROWS = 512
PART = 256


def silu_parts(gate_value):
    sigmoid_gate = jax.nn.sigmoid(gate_value)
    return (gate_value * sigmoid_gate, sigmoid_gate * (1.0 + gate_value * (1.0 - sigmoid_gate)))


def contract_first(left, right):
    return lax.dot_general(
        left, right, (((0,), (0,)), ((), ())), preferred_element_type=jnp.float32
    )


def dot(left, right):
    return jnp.dot(left, right, preferred_element_type=jnp.float32)


def dot_exact(left, right):
    return jnp.dot(
        left, right, precision=lax.Precision.HIGHEST, preferred_element_type=jnp.float32
    )


def contract_last(left, right):
    return lax.dot_general(
        left,
        right,
        (((1,), (1,)), ((), ())),
        precision=lax.Precision.HIGHEST,
        preferred_element_type=jnp.float32,
    )


def keys_kernel(
    mine_ref,
    theirs_ref,
    cot_ref,
    lin_hbm,
    w_ref,
    gate_ref,
    up_ref,
    pi_hbm,
    pg_hbm,
    pu_hbm,
    out_ref,
    perm,
    mask,
    spare,
    packed,
    gate_up_spare,
    lin,
    pi,
    pg,
    pu,
    inp,
    held,
    wbuf,
    acc,
    gate_mul,
    up_mul,
    stage,
    irecv,
    iall,
    ipacked,
    frows,
    frecv,
    fall,
    keys,
    w_sem,
    stage_sem,
    load_sem,
    recv_sem,
    own_send,
    x_send,
    z_send,
    extra_send,
    isem_s,
    isem_r,
    jsem_s,
    jsem_r,
    fsem_s,
    fsem_r,
    ksem_s,
    ksem_r,
    dsem_s,
    dsem_r,
):
    feats, slots_all = cot_ref.shape
    hidden = w_ref.shape[0]
    toks = packed.shape[1]
    seqs = mine_ref.shape[1]
    length = slots_all // seqs
    rank = pg.shape[0]
    depth = feats // PIECES
    wide = feats // PAIRS
    per_pair = PIECES // PAIRS
    tiles = hidden // ROWS
    me = lax.axis_index("tensor")
    core = lax.axis_index("dp")
    z, x = me // 2, me % 2
    other = 1 - x
    o1 = z - 1 + 2 * ((3 - z) // 3)
    o3 = 3 * (1 - z // 2)
    o2 = 6 - z - o1 - o3
    across = {"tensor": z * 2 + other}
    peer = {"dp": 1 - core}

    order = [
        me,
        o1 * 2 + x,
        z * 2 + other,
        o2 * 2 + x,
        o1 * 2 + other,
        o3 * 2 + x,
        o2 * 2 + other,
        o3 * 2 + other,
    ]
    steps = [(shard, pair) for shard in range(8) for pair in range(PAIRS)]

    def w_copy(step):
        index, pair = steps[step]
        start = pl.multiple_of(order[index] * feats + pair * wide, wide)
        return pltpu.make_async_copy(
            w_ref.at[:, pl.ds(start, wide)], wbuf.at[step % W_SLOTS], w_sem.at[step % W_SLOTS]
        )

    loads = [
        pltpu.make_async_copy(source, target, load_sem.at[i])
        for i, (source, target) in enumerate(
            ((lin_hbm, lin), (pi_hbm, pi), (pg_hbm, pg), (pu_hbm, pu))
        )
    ]

    def stage_copy(which, tile):
        ref = [gate_ref, up_ref][which]
        return pltpu.make_async_copy(
            ref.at[pl.ds(tile * ROWS, ROWS)], stage.at[which, tile % 2], stage_sem.at[which, tile % 2]
        )

    loads[0].start()
    loads[1].start()
    for step in range(W_SLOTS):
        w_copy(step).start()
    loads[2].start()
    loads[3].start()
    for which in range(2):
        stage_copy(which, 0).start()

    barrier = pltpu.get_barrier_semaphore()
    for shift in range(1, 8):
        pl.semaphore_signal(
            barrier, inc=1, device_id={"tensor": (me + shift) % 8}, device_id_type=MESH
        )
    pl.semaphore_signal(barrier, inc=1, device_id=peer, device_id_type=MESH)

    def remote(src, dst, send, recv, where):
        return pltpu.make_async_remote_copy(
            src_ref=src,
            dst_ref=dst,
            send_sem=send,
            recv_sem=recv,
            device_id=where,
            device_id_type=MESH,
        )

    def lengths_of(ref):
        return [ref[2, s] for s in range(seqs)]

    def plan(ref):
        long = lengths_of(ref)
        count = sum(long[1:], long[0])
        spill = jnp.maximum(count - toks, 0)
        kept = long[:-1] + [long[-1] - spill]
        starts = [jnp.int32(0)]
        for value in long[:-1]:
            starts.append(starts[-1] + value)
        return long, count, spill, kept, starts

    def make_perm(view, own, far):
        long, count, spill, kept, starts = plan(own)
        far_long, _, far_spill, far_kept, _ = plan(far)
        row = lax.broadcasted_iota(jnp.int32, (length, toks), 0)
        gap = lax.broadcasted_iota(jnp.int32, (length, toks), 1) - row
        for s in range(seqs):
            hit = jnp.logical_and(gap == starts[s], row < kept[s])
            perm[view, pl.ds(s * length, length), :] = jnp.where(hit, 1.0, 0.0).astype(BF16)
        hit = jnp.logical_and(
            gap == count - far_kept[-1],
            jnp.logical_and(row >= far_kept[-1], row < far_long[-1]),
        )
        perm[view, pl.ds(slots_all, length), :] = jnp.where(hit, 1.0, 0.0).astype(BF16)

    def make_mask(view, own, far):
        long, count, spill, kept, starts = plan(own)
        far_long, _, far_spill, _, _ = plan(far)
        column = lax.broadcasted_iota(jnp.int32, (seqs, toks), 1)
        wanted = lax.broadcasted_iota(jnp.int32, (seqs, toks), 0) + core * seqs
        entries = [
            (starts[s], kept[s], long[s], own[0, s]) for s in range(seqs)
        ] + [(count, far_spill, far_long[-1], far[0, seqs - 1])]
        value = jnp.zeros((seqs, toks), F32)
        for first, many, full, slot in entries:
            hit = jnp.logical_and(column >= first, column < first + many)
            hit = jnp.logical_and(hit, wanted == slot)
            scale = lax.rsqrt(jnp.full((seqs, toks), full, jnp.int32).astype(F32))
            value = value + jnp.where(hit, scale, 0.0)
        mask[view] = value

    last = pl.ds(slots_all - length, length)
    make_perm(0, mine_ref, theirs_ref)
    pl.semaphore_wait(barrier, 8)

    c_swap = remote(cot_ref.at[:, last], spare, dsem_s.at[0], dsem_r.at[0], peer)
    c_swap.start()
    g_swaps = [
        remote(ref.at[:, last], gate_up_spare.at[i], dsem_s.at[1 + i], dsem_r.at[1 + i], peer)
        for i, ref in enumerate((gate_ref, up_ref))
    ]

    def own_copy(piece, way):
        where = [
            across,
            {"tensor": jnp.minimum(me + 2, 6 + x)},
            {"tensor": jnp.maximum(me - 2, x)},
        ][way]
        return remote(
            packed.at[pl.ds(piece * depth, depth)],
            held.at[me, pl.ds(piece * depth, depth)],
            own_send.at[way, piece],
            recv_sem.at[me, piece],
            where,
        )

    def block_copy(shard, piece, send, where):
        block = held.at[shard, pl.ds(piece * depth, depth)]
        return remote(block, block, send, recv_sem.at[shard, piece], where)

    def x_copy(k, shard, piece):
        return block_copy(shard, piece, x_send.at[k, piece], across)

    def z_forward(k, piece, act):
        source = [o1, o2, o3][k]
        for way, holds in (
            (1, jnp.logical_and(source < z, z < 3)),
            (-1, jnp.logical_and(source > z, z > 0)),
        ):

            @pl.when(holds)
            def _():
                act(
                    block_copy(
                        source * 2 + x, piece, z_send.at[k, piece], {"tensor": me + 2 * way}
                    )
                )

    def extra_forward(piece, act):
        for i, (way, holds) in enumerate(((1, z < 3), (-1, z == 1))):

            @pl.when(holds)
            def _():
                act(
                    block_copy(
                        z * 2 + other, piece, extra_send.at[i, piece], {"tensor": me + 2 * way}
                    )
                )

    def own_moves(piece, act):
        act(own_copy(piece, 0))

        @pl.when(z < 3)
        def _():
            act(own_copy(piece, 1))

        @pl.when(z > 0)
        def _():
            act(own_copy(piece, 2))

    def start(copy):
        copy.start()

    def wait_send(copy):
        copy.wait_send()

    c_swap.wait_recv()
    for piece in range(PIECES):
        rows = pl.ds(piece * depth, depth)
        packed[rows, :] = (
            dot(cot_ref[rows, :], perm[0, pl.ds(0, slots_all), :])
            + dot(spare[rows, :], perm[0, pl.ds(slots_all, length), :])
        ).astype(BF16)
        own_moves(piece, start)
    for swap in g_swaps:
        swap.start()

    loads[0].wait()
    loads[1].wait()
    inp[...] = dot(pi[...], lin[...])

    def i_copy(shift):
        to = (me + shift) % 8
        return remote(
            inp.at[pl.ds(pl.multiple_of(to * 8, 8), 8)],
            irecv.at[shift - 1],
            isem_s.at[shift - 1],
            isem_r.at[shift - 1],
            {"tensor": to},
        )

    for shift in range(1, 8):
        i_copy(shift).start()

    def multiply(step, first=False):
        index, pair = steps[step]
        block = packed if index == 0 else held.at[order[index]]
        w_copy(step).wait()

        @pl.loop(0, 2)
        def _(tile):
            rows = pl.ds(pl.multiple_of(tile * (hidden // 2), 256), hidden // 2)
            part = dot(wbuf[step % W_SLOTS, rows, :], block[pl.ds(pair * wide, wide), :])
            if first:
                acc[rows, :] = part
            else:
                acc[rows, :] += part

        if step + W_SLOTS < len(steps):
            w_copy(step + W_SLOTS).start()

    def slopes(tile):
        slot = tile % 2
        for which in range(2):
            if tile + 1 < tiles:
                stage_copy(which, tile + 1).start()
            stage_copy(which, tile).wait()

        @pl.loop(0, ROWS // PART)
        def _(part):
            rows = pl.ds(pl.multiple_of(part * PART, PART), PART)
            target = pl.ds(pl.multiple_of(tile * ROWS + part * PART, PART), PART)
            gate_value, up_value = [
                dot(stage[which, slot, rows, :], perm[0, pl.ds(0, slots_all), :])
                + dot(gate_up_spare[which, target, :], perm[0, pl.ds(slots_all, length), :])
                for which in range(2)
            ]
            activated, slope = silu_parts(gate_value)
            gate_mul[target, :] = up_value * slope
            up_mul[target, :] = activated

    for pair in range(PAIRS):
        multiply(pair, first=pair == 0)
    for swap in g_swaps:
        swap.wait_recv()
    for tile in range(3):
        slopes(tile)

    my_rows = pl.ds(pl.multiple_of(me * 8, 8), 8)

    def j_copy(shift):
        block = iall.at[core, my_rows]
        return remote(
            block,
            block,
            jsem_s.at[shift - 1],
            jsem_r.at[shift - 1],
            {"tensor": (me + shift) % 8},
        )

    for index in range(1, 8):
        if index == 3:
            for shift in range(1, 8):
                i_copy(shift).wait_recv()
            total = inp[my_rows, :]
            for shift in range(1, 8):
                total = total + irecv[shift - 1]
            iall[core, my_rows, :] = total
            for shift in range(1, 8):
                j_copy(shift).start()
            make_perm(1, theirs_ref, mine_ref)
            make_mask(0, mine_ref, theirs_ref)
            make_mask(1, theirs_ref, mine_ref)
        if index == 4:
            for shift in range(1, 8):
                j_copy(shift).wait_recv()
            i_swap = remote(iall.at[core], iall.at[core], dsem_s.at[3], dsem_r.at[3], peer)
            i_swap.start()
        if index == 6:
            i_swap.wait_recv()
            for view, near in ((0, core), (1, 1 - core)):
                ipacked[view] = dot_exact(
                    iall[near], perm[view, pl.ds(0, slots_all), :].astype(F32)
                ) + dot_exact(
                    iall[1 - near, :, pl.ds(slots_all - length, length)],
                    perm[view, pl.ds(slots_all, length), :].astype(F32),
                )
        shard = order[index]
        for pair in range(PAIRS):
            for piece in range(pair * per_pair, (pair + 1) * per_pair):
                block_copy(shard, piece, own_send.at[0, piece], across).wait_recv()
                if index in (1, 3, 5):
                    k = index // 2
                    z_forward(k, piece, start)
                    if k > 0 or piece < PIECES // 2:
                        x_copy(k, shard, piece).start()
                if index == 2 and piece >= PIECES // 2:
                    extra_forward(piece, start)
            multiply(index * PAIRS + pair)
        if index <= 2:
            slopes(1 + 2 * index)
            slopes(2 + 2 * index)

    loads[2].wait()
    loads[3].wait()
    gate_sum = jnp.zeros((rank, toks), F32)
    up_sum = jnp.zeros((rank, toks), F32)
    for tile in range(tiles):
        rows = pl.ds(tile * ROWS, ROWS)
        grad = acc[rows, :]
        gate_grad = (grad * gate_mul[rows, :]).astype(BF16)
        up_grad = (grad * up_mul[rows, :]).astype(BF16)
        gate_sum = gate_sum + dot(pg[:, rows], gate_grad)
        up_sum = up_sum + dot(pu[:, rows], up_grad)
    frows[pl.ds(0, rank), :] = gate_sum
    frows[pl.ds(rank, rank), :] = up_sum

    def f_copy(shift):
        to = (me + shift) % 8
        return remote(
            frows.at[pl.ds(pl.multiple_of(to * 16, 16), 16)],
            frecv.at[shift - 1],
            fsem_s.at[shift - 1],
            fsem_r.at[shift - 1],
            {"tensor": to},
        )

    for shift in range(1, 8):
        f_copy(shift).start()
    summed = frows[pl.ds(pl.multiple_of(me * 16, 16), 16), :]
    for shift in range(1, 8):
        f_copy(shift).wait_recv()
        summed = summed + frecv[shift - 1]
    fall[core] = summed
    f_swap = remote(fall.at[core], fall.at[core], dsem_s.at[4], dsem_r.at[4], peer)
    f_swap.start()
    f_swap.wait_recv()

    for s in range(seqs):
        value = jnp.zeros((16, rank), F32)
        for view, near in ((0, core), (1, 1 - core)):
            value = value + contract_last(
                fall[near] * mask[view, pl.ds(s, 1), :], ipacked[view]
            )
        keys[me, pl.ds(s * 16, 16), :] = value.astype(BF16)

    def k_copy(shift):
        block = keys.at[me]
        return remote(
            block,
            block,
            ksem_s.at[shift - 1],
            ksem_r.at[shift - 1],
            {"tensor": (me + shift) % 8},
        )

    for shift in range(1, 8):
        k_copy(shift).start()

    for swap in [c_swap, i_swap, f_swap] + g_swaps:
        swap.wait_send()
    for piece in range(PIECES):
        own_moves(piece, wait_send)
        if piece >= PIECES // 2:
            extra_forward(piece, wait_send)
        for k, source in enumerate((o1, o2, o3)):
            z_forward(k, piece, wait_send)
            if k > 0 or piece < PIECES // 2:
                x_copy(k, source * 2 + x, piece).wait_send()
    for shift in range(1, 8):
        i_copy(shift).wait_send()
        j_copy(shift).wait_send()
        f_copy(shift).wait_send()

    for shift in range(1, 8):
        k_copy(shift).wait_recv()
    for t in range(8):
        for s in range(seqs):
            out_ref[s, pl.ds(t * 16, 16), :] = keys[t, pl.ds(s * 16, 16), :]
    for shift in range(1, 8):
        k_copy(shift).wait_send()


def fused_keys(mine, theirs, cotangent, layer_input, down_weight, gate_pre, up_pre, pi, pg, pu):
    feats, slots_all = cotangent.shape
    hidden, width = down_weight.shape
    rank = pg.shape[0]
    seqs = mine.shape[1]
    length = slots_all // seqs
    toks = slots_all - length
    smem = pl.BlockSpec(memory_space=pltpu.SMEM)
    vmem = pl.BlockSpec(memory_space=pltpu.VMEM)
    hbm = pl.BlockSpec(memory_space=pl.ANY)
    sems = pltpu.SemaphoreType.DMA
    return pl.pallas_call(
        keys_kernel,
        out_shape=jax.ShapeDtypeStruct((seqs, 2 * rank, rank), BF16),
        in_specs=[smem, smem, vmem] + [hbm] * 7,
        out_specs=vmem,
        scratch_shapes=[
            pltpu.VMEM((2, slots_all + length, toks), BF16),
            pltpu.VMEM((2, seqs, toks), F32),
            pltpu.VMEM((feats, length), BF16),
            pltpu.VMEM((feats, toks), BF16),
            pltpu.VMEM((2, hidden, length), BF16),
            pltpu.VMEM((feats, slots_all), BF16),
            pltpu.VMEM((rank, feats), BF16),
            pltpu.VMEM((rank, hidden), BF16),
            pltpu.VMEM((rank, hidden), BF16),
            pltpu.VMEM((rank, slots_all), F32),
            pltpu.VMEM((8, feats, toks), BF16),
            pltpu.VMEM((W_SLOTS, hidden, feats // PAIRS), BF16),
            pltpu.VMEM((hidden, toks), F32),
            pltpu.VMEM((hidden, toks), F32),
            pltpu.VMEM((hidden, toks), F32),
            pltpu.VMEM((2, 2, ROWS, slots_all), BF16),
            pltpu.VMEM((7, 8, slots_all), F32),
            pltpu.VMEM((2, rank, slots_all), F32),
            pltpu.VMEM((2, rank, toks), F32),
            pltpu.VMEM((2 * rank, toks), F32),
            pltpu.VMEM((7, 16, toks), F32),
            pltpu.VMEM((2, 16, toks), F32),
            pltpu.VMEM((8, seqs * 16, rank), BF16),
            sems((W_SLOTS,)),
            sems((2, 2)),
            sems((4,)),
            sems((8, PIECES)),
            sems((3, PIECES)),
            sems((3, PIECES)),
            sems((3, PIECES)),
            sems((2, PIECES)),
        ]
        + [sems((7,))] * 8
        + [sems((5,))] * 2,
        compiler_params=pltpu.CompilerParams(
            collective_id=0, has_side_effects=True, vmem_limit_bytes=60 * 2**20
        ),
        cost_estimate=pl.CostEstimate(
            flops=2 * hidden * width * toks,
            bytes_accessed=2 * hidden * (width + 2 * slots_all),
            transcendentals=hidden * toks,
        ),
    )(mine, theirs, cotangent, layer_input, down_weight, gate_pre, up_pre, pi, pg, pu)


def per_device_fused(
    cotangent,
    layer_input,
    gate_pre,
    up_pre,
    down_weight,
    proj_input,
    proj_gate,
    proj_up,
    store_slot,
    example_ids,
    lengths,
):
    rank = proj_gate.shape[1]
    seqs = lengths.shape[0]
    core = lax.axis_index("dp")
    mine = jnp.stack([store_slot, example_ids, lengths])
    theirs = lax.ppermute(mine, "dp", [(0, 1), (1, 0)])
    wanted = core * seqs + jnp.arange(seqs, dtype=jnp.int32)
    both = jnp.concatenate([mine, theirs], axis=1)
    chosen = both[0][None, :] == wanted[:, None]
    store_ids = jnp.sum(jnp.where(chosen, both[1][None, :], 0), axis=1).astype(jnp.int32)
    keys = fused_keys(
        mine,
        theirs,
        cotangent,
        layer_input,
        down_weight,
        gate_pre,
        up_pre,
        proj_input.T,
        proj_gate.T,
        proj_up.T,
    )
    return (keys.reshape(seqs, 2 * rank * rank), store_ids)


def per_device_plain(
    cotangent,
    layer_input,
    gate_pre,
    up_pre,
    down_weight,
    proj_input,
    proj_gate,
    proj_up,
    store_slot,
    example_ids,
    lengths,
):
    tok_count = cotangent.shape[1]
    proj_rank = proj_gate.shape[1]
    seq_count = lengths.shape[0]
    seq_len = tok_count // seq_count
    hidden_grad = jnp.dot(
        down_weight,
        lax.all_gather(cotangent, "tensor", axis=0, tiled=True),
        preferred_element_type=jnp.float32,
    )
    input_partial = contract_first(proj_input, layer_input)
    gate_value = gate_pre.astype(jnp.float32)
    up_value = up_pre.astype(jnp.float32)
    activated, slope = silu_parts(gate_value)
    gate_grad = (hidden_grad * up_value * slope).astype(jnp.bfloat16)
    up_grad = (hidden_grad * activated).astype(jnp.bfloat16)
    gate_factor = contract_first(proj_gate, gate_grad)
    up_factor = contract_first(proj_up, up_grad)
    partial_rows = jnp.concatenate([gate_factor, up_factor, input_partial], axis=0)
    inverse_root = lax.rsqrt(lengths.astype(jnp.float32))
    summed = lax.psum(partial_rows, "tensor")
    input_factor = summed[2 * proj_rank :]
    position = jnp.arange(seq_len, dtype=jnp.int32)
    inside = jnp.where(position[None, :] < lengths[:, None], 1.0, 0.0).astype(jnp.float32)
    weight = inside * inverse_root[:, None]
    grads_three = summed[: 2 * proj_rank].reshape(2, proj_rank, seq_count, seq_len)
    inputs_three = input_factor.reshape(proj_rank, seq_count, seq_len)
    key_values = jnp.einsum(
        "gael,bel,el->egab", grads_three, inputs_three, weight, precision=lax.Precision.HIGHEST
    )
    key_values = key_values.reshape(seq_count, -1)
    key_rows = key_values.astype(jnp.bfloat16)
    dp_count = lax.axis_size("dp")
    slot_index = jnp.arange(dp_count * seq_count, dtype=jnp.int32)
    chosen = store_slot[None, :] == slot_index[:, None]
    outgoing = jnp.dot(
        chosen.astype(jnp.bfloat16), key_rows, preferred_element_type=jnp.float32
    ).astype(jnp.bfloat16)
    outgoing = outgoing.reshape(dp_count, seq_count, -1)
    outgoing_ids = jnp.sum(jnp.where(chosen, example_ids[None, :], 0), axis=1).reshape(
        dp_count, seq_count
    )
    arrived, arrived_ids = (
        lax.all_to_all(outgoing, "dp", split_axis=0, concat_axis=0, tiled=True),
        lax.all_to_all(outgoing_ids, "dp", split_axis=0, concat_axis=0, tiled=True),
    )
    store_keys = jnp.sum(arrived.astype(jnp.float32), axis=0).astype(jnp.bfloat16)
    store_ids = jnp.sum(arrived_ids, axis=0).astype(jnp.int32)
    return (store_keys, store_ids)


def solution(mesh):
    placed = (
        P("tensor", ("parts", "dp")),
        P("tensor", ("parts", "dp")),
        P("tensor", ("parts", "dp")),
        P("tensor", ("parts", "dp")),
        P("tensor", None),
        P("tensor", None),
        P("tensor", None),
        P("tensor", None),
        P(("parts", "dp")),
        P(("parts", "dp")),
        P(("parts", "dp")),
    )
    fits = mesh.shape["tensor"] == 8 and mesh.shape["dp"] == 2
    return jax.shard_map(
        per_device_fused if fits else per_device_plain,
        mesh=mesh,
        in_specs=placed,
        out_specs=(P(("parts", "dp"), None), P(("parts", "dp"))),
        check_vma=False,
    )
```
